32 devices in a mesh: groups: 2 (over x), tok: 16 (over z, y, core).
Axes of the slice: x: 2, y: 2, z: 4, core: 2. Of those that a mesh axis runs over, the one named last changes fastest.
Arguments:
- queries: bfloat16 [4096, 2048], P(('groups', 'tok')), parts along dimension 0, may hold values from -6 to 6
- key_rows: bfloat16 [4096, 2048], P(('groups', 'tok')), parts along dimension 0, may hold values from -6 to 6
- value_rows: bfloat16 [4096, 2048], P(('groups', 'tok')), parts along dimension 0, may hold values from -6 to 6
- step_size: bfloat16 [4096, 16], P(('groups', 'tok')), parts along dimension 0, may hold values from 0.099609375 to 1
- routes: int32 [4096, 2], P(('groups', 'tok')), parts along dimension 0, may hold values from 0 to 7, all different within a row; in each aligned block of 128 rows (0 to 127, 128 to 255, ...) at most 64 rows name the same one
- route_weight: float32 [4096, 2], P(('groups', 'tok')), parts along dimension 0, may hold values from 0.2 to 1
- init_state: float32 [128, 128, 128], P('tok'), may hold values from -0.5 to 0.5
Outputs:
- layer_out: bfloat16 [4096, 2048], P(('groups', 'tok')), parts along dimension 0
The draws below stay inside these ranges and needn't reach their ends.
There are 2 independent parts, one for each index of `groups`. The reference program is written for one: setup_inputs(seed, part) draws one part's arguments, and reference() takes and returns one part's arrays. A program takes and returns all parts, laid end to end along the dimension named above; an argument that names none is the same for every part. Nothing has to cross between parts.
Inputs may be any that keep to these rules, and one draw needn't show every extreme that they name: `routes`: each row names two different memories. Among the 128 rows of one device no memory is named by more than 64 rows, a bound that some block reaches.
All inputs are finite; a program needn't handle non-finite values.
Results may differ from the reference program's by a relative error of at most 0.0055.
Values may be sent and summed in bfloat16 or wider, within the bound.
A program may use at most 128 MiB of HBM per device.

```python
import math
import jax
import jax.numpy as jnp
import numpy as np
from jax import lax

MEM = 8
H = 16
DK = 128
D = 2048
TOK_DEV = 128
ITERS = 3
TOKENS = 2048
MOST = 64


def levels(key, shape, shards, least, high):
    def one(dim, shards_of):
        heights = jax.random.uniform(jax.random.fold_in(jax.random.fold_in(key, 6), dim), (shards_of,), jnp.float32, least / len(shards), high / len(shards))
        return jnp.repeat(jnp.exp(heights), shape[dim] // shards_of).reshape((-1,) + (1,) * (len(shape) - dim - 1))

    loudness = one(*shards[0])
    for cut in shards[1:]:
        loudness = loudness * one(*cut)
    return loudness


def shared_out(stream_key, own, number, rows, count, top, limit, lean):
    sequence = jax.random.permutation(stream_key, count)
    crowded, common = portions_of(count, rows * top, limit, lean, True), portions_of(count, rows * top, limit, lean, False)
    places = jnp.arange(count)

    def named(sizes, rotation):
        used = int((sizes > 0).sum())
        fixed = max(1, used // 4)
        passed = fixed + (places - fixed + rotation * (used - fixed)) % max(1, count - fixed)
        return jnp.zeros((count,), jnp.int32).at[sequence[jnp.where(places < fixed, places, passed)]].set(jnp.asarray(sizes, jnp.int32))

    sizes = jnp.where(number % 4 == 0, named(crowded, number // 4), named(common, number - number // 4 - 1))
    mixed = jax.random.permutation(jax.random.fold_in(own, 3), count)
    donor, sink = mixed[0:count // 2 * 2:2], mixed[1:count // 2 * 2:2]
    room = jnp.minimum(sizes[donor] - 1, limit - sizes[sink]) // 2
    room = jnp.where((donor == sequence[0]) | (sink == sequence[0]) | (sizes[sink] == 0), 0, jnp.maximum(room, 0))
    passed = jax.random.randint(jax.random.fold_in(own, 4), (count // 2,), 0, 1 << 20) % (room + 1)
    sizes = sizes.at[donor].add(-passed).at[sink].add(passed)
    members = jnp.searchsorted(jnp.cumsum(sizes), jnp.arange(rows * top), side="right").astype(jnp.int32)
    table = members.reshape(top, rows).T
    table = table[jax.random.permutation(jax.random.fold_in(own, 1), rows)]
    rotation = jax.random.randint(jax.random.fold_in(own, 2), (rows, 1), 0, top)
    return jnp.take_along_axis(table, (jnp.arange(top)[None, :] + rotation) % top, axis=1)


def portions_of(count, total, reach, skew, full):
    loads = [(1 << 20) // math.isqrt(rank ** skew) + 1 for rank in range(1, count + 1)]
    largest = reach if full else min(reach, max(-(-total // count), total * loads[0] // sum(loads)))
    least = 1 if total - largest >= count - 1 else 0
    counts, rest = [largest] + [least] * (count - 1), total - largest - least * (count - 1)
    while rest > 0:
        candidates = [i for i in range(1, count) if counts[i] < largest] or [i for i in range(1, count) if counts[i] < reach]
        mass, budget = sum([loads[i] for i in candidates]), rest
        for i in candidates:
            addition = min(reach - counts[i], max(1, budget * loads[i] // mass), rest)
            counts[i] = counts[i] + addition
            rest = rest - addition
    return np.array(counts)


def centred(key, extent, scale, limit, pieces=(), kind=jnp.bfloat16):
    loudness = levels(key, extent, pieces, -0.22, 0.18) if pieces else 1.0
    result = jax.random.normal(key, extent, jnp.float32) * scale * loudness
    return jnp.minimum(jnp.maximum(result, -limit), limit).astype(kind)


def setup_inputs(seed: int = 0, part: int = 0) -> dict:
    arg_keys = jax.random.split(jax.random.key(seed), 8)
    part_keys = jax.random.split(jax.random.fold_in(arg_keys[7], part), 8)
    queries = centred(part_keys[0], (TOKENS, D), 1.0, 6.0, ((0, 16),))
    key_rows = centred(part_keys[1], (TOKENS, D), 1.0, 6.0, ((0, 16),))
    value_rows = centred(part_keys[2], (TOKENS, D), 1.0, 6.0, ((0, 16),))
    step_size = jnp.clip(jnp.exp(math.log(1.0) - 2.306499 * jax.random.uniform(part_keys[3], (TOKENS, H), jnp.float32) ** levels(part_keys[3], (TOKENS, H), ((0, 16),), -0.2, 0.2)), 0.099609375, 1.0).astype(jnp.bfloat16)
    routes_keys = jax.random.split(jax.random.fold_in(part_keys[4], 1), TOKENS // TOK_DEV)
    routes_turns = jax.random.permutation(jax.random.fold_in(part_keys[4], 3), TOKENS // TOK_DEV)
    routes = jax.vmap(lambda own, number: shared_out(jax.random.fold_in(part_keys[4], 2), own, number, TOK_DEV, MEM, 2, MOST, 2))(routes_keys, routes_turns).reshape((TOKENS, 2))
    route_weight = jnp.clip(0.2 + 0.8 * jax.random.uniform(part_keys[5], (TOKENS, 2), jnp.float32) ** levels(part_keys[5], (TOKENS, 2), ((0, 16),), -0.2, 0.2), 0.2, 1.0)
    init_state = centred(arg_keys[6], (MEM * H, DK, DK), DK ** -0.5, 0.5, ((0, 16),), jnp.float32)
    return dict(queries=queries, key_rows=key_rows, value_rows=value_rows, step_size=step_size, routes=routes, route_weight=route_weight, init_state=init_state)


def reference(queries, key_rows, value_rows, step_size, routes, route_weight, init_state):
    tokens = queries.shape[0]
    raw_keys = key_rows.astype(jnp.float32).reshape(tokens, H, DK)
    normalized_keys = raw_keys / jnp.sqrt(lax.optimization_barrier(jnp.sum(raw_keys * raw_keys, axis=-1, keepdims=True)) + 1e-06)
    target_values = value_rows.astype(jnp.float32).reshape(tokens, H, DK)
    query_head_rows = queries.astype(jnp.float32).reshape(tokens, H, DK)
    rates = step_size.astype(jnp.float32)
    step_scale = 4.0 / math.sqrt(TOKENS)
    layer_out = jnp.zeros((tokens, H, DK), jnp.float32)
    for memory in range(MEM):
        matched = routes == memory
        picked = lax.optimization_barrier(jnp.sum(matched.astype(jnp.float32), axis=1))
        weight = lax.optimization_barrier(jnp.sum(jnp.where(matched, route_weight, jnp.zeros_like(route_weight)), axis=1))
        weighted_output = normalized_keys * (rates * picked[:, None])[:, :, None]
        memory_state = init_state[memory * H:(memory + 1) * H]
        for iteration in range(ITERS):
            residual_error = target_values - jnp.einsum('nlz,lzi->nli', normalized_keys, memory_state, precision=lax.Precision.HIGHEST)
            memory_gradient = jnp.einsum('wpb,wpi->pbi', weighted_output, residual_error, precision=lax.Precision.HIGHEST)
            memory_state = memory_state + step_scale * memory_gradient
        closing_state = memory_state.astype(jnp.bfloat16).astype(jnp.float32)
        routed_tokens = jnp.einsum('nlz,lzi->nli', query_head_rows, closing_state, precision=lax.Precision.HIGHEST)
        routed_tokens = lax.optimization_barrier(routed_tokens.astype(jnp.bfloat16)).astype(jnp.float32)
        layer_out = layer_out + weight[:, None, None] * routed_tokens
    return layer_out.reshape(tokens, H * DK).astype(jnp.bfloat16)
```

```python
import functools
import math

import jax
import jax.numpy as jnp
from jax import lax
from jax.experimental import pallas as pl
from jax.experimental.pallas import tpu as pltpu
from jax.sharding import PartitionSpec as P

MEM = 8
H = 16
DK = 128
ITERS = 3
MESH = pl.DeviceIdType.MESH
F32 = jnp.float32
BF16 = jnp.bfloat16


def split(x):
    high = x.astype(BF16)
    return high, (x - high.astype(F32)).astype(BF16)


def kernel(
    n, scale, q_ref, k_ref, v_ref, meta_ref, init_ref, out_ref,
    kv_buf, meta_buf, q_buf, init_buf, acc, final, res,
    kv_sem, meta_sem, q_sem, init_sem, out_sem,
    kv_send, meta_send, q_send, init_send, out_send, own_sem,
):
    per_dev = MEM * H // n
    blocks = H // per_dev
    group = lax.axis_index("groups")
    me = lax.axis_index("tok")
    memory_of_me = me // blocks
    place = me % H
    first = me - place

    def head_of(p):
        return (p % blocks) * per_dev + (p // blocks) % per_dev

    def columns(h):
        return pl.ds(pl.multiple_of(h * DK, DK), DK)

    def offset(i, count):
        return count // 2 + (1 - 2 * (i % 2)) * ((i + 1) // 2)

    def remote(src, dst, send, recv, p):
        return pltpu.make_async_remote_copy(
            src_ref=src, dst_ref=dst, send_sem=send, recv_sem=recv,
            device_id=(group, p), device_id_type=MESH,
        )

    barrier = pltpu.get_barrier_semaphore()

    def greet(i, c):
        pl.semaphore_signal(
            barrier, inc=1, device_id=(group, (me + 1 + i) % n), device_id_type=MESH
        )
        return c

    lax.fori_loop(0, n - 1, greet, 0)

    my_head = head_of(me)
    own = [
        pltpu.make_async_copy(k_ref.at[:, columns(my_head)], kv_buf.at[me, 0], own_sem.at[0]),
        pltpu.make_async_copy(v_ref.at[:, columns(my_head)], kv_buf.at[me, 1], own_sem.at[1]),
        pltpu.make_async_copy(q_ref.at[:, columns(my_head)], q_buf.at[place], own_sem.at[2]),
        pltpu.make_async_copy(
            init_ref.at[memory_of_me % per_dev], init_buf.at[memory_of_me], own_sem.at[3]
        ),
        pltpu.make_async_copy(meta_ref.at[my_head], meta_buf.at[me], own_sem.at[4]),
    ]
    for copy in own:
        copy.start()
    pl.semaphore_wait(barrier, n - 1)

    def send_kv(i, c):
        p = (me + offset(i, n)) % n
        h = head_of(p)
        remote(meta_ref.at[h], meta_buf.at[me], meta_send, meta_sem, p).start()
        remote(k_ref.at[:, columns(h)], kv_buf.at[me, 0], kv_send, kv_sem.at[me], p).start()
        remote(v_ref.at[:, columns(h)], kv_buf.at[me, 1], kv_send, kv_sem.at[me], p).start()
        return c

    lax.fori_loop(0, n - 1, send_kv, 0)

    def send_init(i, c):
        to = (memory_of_me + offset(i, MEM)) % MEM
        remote(
            init_ref.at[to % per_dev], init_buf.at[memory_of_me], init_send, init_sem,
            to * blocks + me % blocks,
        ).start()
        return c

    lax.fori_loop(0, MEM - 1, send_init, 0)

    def send_q(i, c):
        p = first + (place + offset(i, H)) % H
        remote(
            q_ref.at[:, columns(head_of(p))], q_buf.at[place], q_send, q_sem.at[place], p
        ).start()
        return c

    lax.fori_loop(0, H - 1, send_q, 0)

    for copy in own:
        copy.wait()
    others = meta_buf.at[pl.ds(0, n - 1)]
    remote(others, others, meta_send, meta_sem, me).wait_recv()
    memories = lax.broadcasted_iota(jnp.int32, (MEM, DK), 0).astype(F32)

    def gradient(source, fresh):
        meta = meta_buf[source]
        picked = (meta[1:2] == memories) | (meta[2:3] == memories)
        keys = kv_buf[source, 0].astype(F32)
        keys_t = keys.T
        inverse_row = 1.0 / jnp.sqrt(jnp.sum(keys_t * keys_t, axis=0, keepdims=True) + 1e-06)
        inverse_col = 1.0 / jnp.sqrt(jnp.sum(keys * keys, axis=1, keepdims=True) + 1e-06)
        unit_t = keys_t * (inverse_row * meta[0:1])
        rate = picked.astype(F32)
        unit, unit_low = split(keys * inverse_col)
        right = jnp.concatenate([unit, kv_buf[source, 1]], axis=1)
        right = jnp.concatenate([right, right], axis=0)
        high, low = split(unit_t)
        for m in range(MEM):
            mask = rate[m : m + 1].astype(BF16)
            both = jnp.concatenate([high * mask, low * mask], axis=1)
            part = jnp.dot(both, right, preferred_element_type=F32)
            rows = pl.ds(m * DK, DK)
            acc[rows, :] = part if fresh else acc[rows, :] + part
            acc[rows, 0:DK] = acc[rows, 0:DK] + jnp.dot(
                high * mask, unit_low, preferred_element_type=F32
            )

    gradient(me, True)

    def arrive(i, c):
        source = (me + n - offset(i, n)) % n
        slot = kv_buf.at[source]
        remote(slot, slot, kv_send, kv_sem.at[source], me).wait_recv()
        gradient(source, False)
        return c

    lax.fori_loop(0, n - 1, arrive, 0)

    others = init_buf.at[pl.ds(0, MEM - 1)]
    remote(others, others, init_send, init_sem, me).wait_recv()
    zero = jnp.zeros((DK, DK), BF16)
    for step in range(ITERS):
        for m in range(MEM):
            rows = pl.ds(m * DK, DK)
            state = init_buf[m]
            left = jnp.concatenate(split(acc[rows, 0:DK]), axis=1)
            high, low = split(state)
            right = jnp.concatenate(
                [jnp.concatenate([high, low], axis=1), jnp.concatenate([high, zero], axis=1)],
                axis=0,
            )
            product = jnp.dot(left, right, preferred_element_type=F32)
            product = product[:, 0:DK] + product[:, DK:]
            state = state + scale * (acc[rows, DK:] - product)
            if step < ITERS - 1:
                init_buf[m] = state
            else:
                final[:, m * DK : (m + 1) * DK] = state.astype(BF16)

    def read_out(source):
        meta = meta_buf[first + source]
        weight = jnp.where(meta[1:2] == memories, meta[3:4], 0.0) + jnp.where(
            meta[2:3] == memories, meta[4:5], 0.0
        )
        weight = jnp.concatenate([weight, jnp.zeros((DK - MEM, DK), F32)], axis=0).T
        routed = jnp.dot(q_buf[source], final[...], preferred_element_type=F32)
        total = jnp.zeros((DK, DK), F32)
        for m in range(MEM):
            piece = routed[:, m * DK : (m + 1) * DK].astype(BF16).astype(F32)
            total = total + weight[:, m : m + 1] * piece
        res[source] = total.astype(BF16)

    read_out(place)
    back = pltpu.make_async_copy(res.at[place], out_ref.at[:, columns(my_head)], own_sem.at[0])
    back.start()

    def answer(i, c):
        source = (place + H - offset(i, H)) % H
        slot = q_buf.at[source]
        remote(slot, slot, q_send, q_sem.at[source], me).wait_recv()
        read_out(source)
        remote(
            res.at[source], out_ref.at[:, columns(my_head)], out_send, out_sem, first + source
        ).start()
        return c

    lax.fori_loop(0, H - 1, answer, 0)

    back.wait()
    others = q_buf.at[pl.ds(0, H - 1)]
    remote(others, others, out_send, out_sem, me).wait()
    remote(others, others, q_send, q_sem.at[place], me).wait_send()
    others = kv_buf.at[pl.ds(0, n - 1)]
    remote(others, others, kv_send, kv_sem.at[me], me).wait_send()
    others = meta_buf.at[pl.ds(0, n - 1)]
    remote(others, others, meta_send, meta_sem, me).wait_send()
    others = init_buf.at[pl.ds(0, MEM - 1)]
    remote(others, others, init_send, init_sem, me).wait_send()


def on_device(queries, key_rows, value_rows, step_size, routes, route_weight, init_state):
    n = lax.axis_size("tok")
    rows = queries.shape[0]
    scale = 4.0 / math.sqrt(rows * n)
    rates = step_size.T.astype(F32)[:, None, :]
    shared = jnp.concatenate(
        [routes.T.astype(F32), route_weight.T, jnp.zeros((3, rows), F32)], axis=0
    )
    meta = jnp.concatenate([rates, jnp.broadcast_to(shared, (H, 7, rows))], axis=1)
    dma = pltpu.SemaphoreType.DMA
    return pl.pallas_call(
        functools.partial(kernel, n, scale),
        out_shape=jax.ShapeDtypeStruct(queries.shape, BF16),
        in_specs=[pl.BlockSpec(memory_space=pl.ANY)] * 3
        + [pl.BlockSpec(memory_space=pltpu.VMEM)]
        + [pl.BlockSpec(memory_space=pl.ANY)],
        out_specs=pl.BlockSpec(memory_space=pltpu.VMEM),
        scratch_shapes=[
            pltpu.VMEM((n, 2, rows, DK), BF16),
            pltpu.VMEM((n, 8, rows), F32),
            pltpu.VMEM((H, rows, DK), BF16),
            pltpu.VMEM((MEM, DK, DK), F32),
            pltpu.VMEM((MEM * DK, 2 * DK), F32),
            pltpu.VMEM((DK, MEM * DK), BF16),
            pltpu.VMEM((H, rows, DK), BF16),
            dma((n,)), dma, dma((H,)), dma, dma,
            dma, dma, dma, dma, dma, dma((5,)),
        ],
        compiler_params=pltpu.CompilerParams(
            collective_id=0, has_side_effects=True, vmem_limit_bytes=40 * 1024 * 1024
        ),
    )(queries, key_rows, value_rows, meta, init_state)


def solution(mesh):
    tokens = P(("groups", "tok"), None)
    return jax.shard_map(
        on_device,
        mesh=mesh,
        in_specs=(tokens,) * 6 + (P("tok", None, None),),
        out_specs=tokens,
        check_vma=False,
    )
```

```python
import functools
import math

import jax
import jax.numpy as jnp
from jax import lax
from jax.experimental import pallas as pl
from jax.experimental.pallas import tpu as pltpu
from jax.sharding import PartitionSpec as P

MEM = 8
H = 16
DK = 128
ITERS = 3
PAIRS = H // 2
OWN = MEM // 2
PACKED = (OWN + OWN // 2) * DK + 16
MESH = pl.DeviceIdType.MESH
F32 = jnp.float32
BF16 = jnp.bfloat16


def split(x):
    high = x.astype(BF16)
    return high, (x - high.astype(F32)).astype(BF16)


def kernel(
    n, scale, q_ref, k_ref, v_ref, meta_ref, init_ref, out_ref,
    kv_buf, meta_buf, q_buf, init_buf, acc, pack_out, pack_in, final, part, res,
    kv_sem, meta_sem, q_sem, init_sem, pack_sem, final_sem, out_sem,
    kv_send, meta_send, q_send, init_send, pack_send, final_send, out_send, own_sem,
):
    per_dev = MEM * H // n
    blocks = H // per_dev
    half = n // 2
    stride = max(1, blocks // 8)
    group = lax.axis_index("groups")
    me = lax.axis_index("tok")
    side = me // half
    base = side * half
    local = me % half
    twin = (me + half) % n
    slot_of_me = local // blocks
    place = (local // stride) % PAIRS
    first = (local // (PAIRS * stride)) * (PAIRS * stride) + local % stride

    def pair_of(l):
        if per_dev >= 2:
            pairs = per_dev // 2
            return (l % blocks) * pairs + (l // blocks) % pairs
        return (l % blocks) // 2

    def columns(h):
        return pl.ds(pl.multiple_of(h * DK, DK), DK)

    def offset(i, count):
        return count // 2 + (1 - 2 * (i % 2)) * ((i + 1) // 2)

    def remote(src, dst, send, recv, p):
        return pltpu.make_async_remote_copy(
            src_ref=src, dst_ref=dst, send_sem=send, recv_sem=recv,
            device_id=(group, p), device_id_type=MESH,
        )

    barrier = pltpu.get_barrier_semaphore()

    def greet(i, c):
        pl.semaphore_signal(
            barrier, inc=1, device_id=(group, base + (local + 1 + i) % half),
            device_id_type=MESH,
        )
        return c

    lax.fori_loop(0, half - 1, greet, 0)
    pl.semaphore_signal(barrier, inc=1, device_id=(group, twin), device_id_type=MESH)

    pair = pair_of(local)
    own = [pltpu.make_async_copy(meta_ref.at[pl.ds(2 * pair, 2)], meta_buf.at[local], own_sem.at[0])]
    for e in range(2):
        here = columns(2 * pair + e)
        own += [
            pltpu.make_async_copy(k_ref.at[:, here], kv_buf.at[e, local, 0], own_sem.at[1 + 3 * e]),
            pltpu.make_async_copy(v_ref.at[:, here], kv_buf.at[e, local, 1], own_sem.at[2 + 3 * e]),
            pltpu.make_async_copy(q_ref.at[:, here], q_buf.at[e, place], own_sem.at[3 + 3 * e]),
        ]
    if per_dev >= 2:
        own.append(
            pltpu.make_async_copy(
                init_ref.at[pl.ds(2 * (slot_of_me % (per_dev // 2)), 2)],
                init_buf.at[pl.ds(2 * slot_of_me, 2)], own_sem.at[7],
            )
        )
    else:
        own.append(
            pltpu.make_async_copy(
                init_ref.at[0], init_buf.at[2 * slot_of_me + local % 2], own_sem.at[7]
            )
        )
    for copy in own:
        copy.start()
    pl.semaphore_wait(barrier, half)

    for e in range(2):
        def send_kv(i, c):
            l = (local + offset(i, half)) % half
            p = base + l
            h = 2 * pair_of(l) + e
            if e == 0:
                remote(
                    meta_ref.at[pl.ds(2 * pair_of(l), 2)], meta_buf.at[local],
                    meta_send, meta_sem, p,
                ).start()
            sem = kv_sem.at[e, local]
            remote(k_ref.at[:, columns(h)], kv_buf.at[e, local, 0], kv_send, sem, p).start()
            remote(v_ref.at[:, columns(h)], kv_buf.at[e, local, 1], kv_send, sem, p).start()
            return c

        lax.fori_loop(0, half - 1, send_kv, 0)

    if per_dev >= 2:
        def send_init(i, c):
            to = (slot_of_me + 1 + i) % OWN
            remote(
                init_ref.at[pl.ds(2 * (to % (per_dev // 2)), 2)],
                init_buf.at[pl.ds(2 * slot_of_me, 2)], init_send, init_sem,
                base + to * blocks + local % blocks,
            ).start()
            return c

        lax.fori_loop(0, OWN - 1, send_init, 0)
        init_slots = init_buf.at[pl.ds(0, 2 * OWN - 2)]
    else:
        mine = 2 * slot_of_me + local % 2

        def send_init(i, c):
            to = (mine + 1 + i) % (2 * OWN)
            remote(
                init_ref.at[0], init_buf.at[mine], init_send, init_sem,
                base + (to // 2) * blocks + (local % blocks) // 2 * 2 + to % 2,
            ).start()
            return c

        lax.fori_loop(0, 2 * OWN - 1, send_init, 0)
        init_slots = init_buf.at[pl.ds(0, 2 * OWN - 1)]

    for e in range(2):
        def send_q(i, c):
            l = first + stride * ((place + offset(i, PAIRS)) % PAIRS)
            remote(
                q_ref.at[:, columns(2 * pair_of(l) + e)], q_buf.at[e, place],
                q_send, q_sem.at[e, place], base + l,
            ).start()
            return c

        lax.fori_loop(0, PAIRS - 1, send_q, 0)

    for copy in own:
        copy.wait()
    meta_slots = meta_buf.at[pl.ds(0, half - 1)]
    remote(meta_slots, meta_slots, meta_send, meta_sem, me).wait_recv()
    memories = lax.broadcasted_iota(jnp.int32, (MEM, DK), 0).astype(F32)
    row = lax.broadcasted_iota(jnp.int32, (DK, DK), 0)
    col = lax.broadcasted_iota(jnp.int32, (DK, DK), 1)

    def gradient(e, source, fresh):
        meta = meta_buf[source, e]
        picked = (meta[1:2] == memories) | (meta[2:3] == memories)
        keys = kv_buf[e, source, 0].astype(F32)
        keys_t = keys.T
        inverse_row = 1.0 / jnp.sqrt(jnp.sum(keys_t * keys_t, axis=0, keepdims=True) + 1e-06)
        inverse_col = 1.0 / jnp.sqrt(jnp.sum(keys * keys, axis=1, keepdims=True) + 1e-06)
        unit = (keys * inverse_col).astype(BF16)
        right = jnp.concatenate([unit, kv_buf[e, source, 1]], axis=1)
        right = jnp.concatenate([right, right], axis=0)
        both = jnp.concatenate(split(keys_t * (inverse_row * meta[0:1])), axis=1)
        rate = picked.astype(F32)
        rate = jnp.concatenate([rate, rate], axis=1).astype(BF16)
        for m in range(MEM):
            rows = pl.ds(m * DK, DK)
            term = jnp.dot(both * rate[m : m + 1], right, preferred_element_type=F32)
            acc[e, rows, :] = term if fresh else acc[e, rows, :] + term

    away = (1 - side) * (OWN * DK)
    kept = side * (OWN * DK)

    def rows_at(start, m):
        return pl.ds(pl.multiple_of(start + m * DK, DK), DK)

    for e in range(2):
        gradient(e, local, True)

        def arrive(i, c):
            source = (local + half - offset(i, half)) % half
            slot = kv_buf.at[e, source]
            remote(slot, slot, kv_send, kv_sem.at[e, source], me).wait_recv()
            gradient(e, source, False)
            return c

        lax.fori_loop(0, half - 1, arrive, 0)
        for m in range(OWN):
            pack_out[e, m * DK : (m + 1) * DK] = acc[e, rows_at(away, m), DK:].astype(BF16)
        diagonals = []
        for m in range(0, OWN, 2):
            lower = acc[e, rows_at(away, m), 0:DK]
            upper = acc[e, rows_at(away, m + 1), 0:DK]
            at = (OWN + m // 2) * DK
            pack_out[e, at : at + DK] = jnp.where(row >= col, lower, upper).astype(BF16)
            diagonals.append(jnp.sum(jnp.where(row == col, upper, 0.0), axis=0, keepdims=True))
        diagonals.append(jnp.zeros((16 - OWN // 2, DK), F32))
        pack_out[e, PACKED - 16 :] = jnp.concatenate(diagonals, axis=0).astype(BF16)
        remote(
            pack_out.at[e], pack_in.at[e], pack_send.at[e], pack_sem.at[e], twin
        ).start()

    remote(init_slots, init_slots, init_send, init_sem, me).wait_recv()
    zero = jnp.zeros((DK, DK), BF16)
    for e in range(2):
        remote(pack_out.at[e], pack_in.at[e], pack_send.at[e], pack_sem.at[e], twin).wait()
        diagonals = pack_in[e, PACKED - 16 :].astype(F32)
        lefts, targets, states = [], [], []
        for m in range(OWN):
            at = (OWN + m // 2) * DK
            packed = pack_in[e, at : at + DK].astype(F32)
            if m % 2 == 0:
                other = jnp.where(row >= col, packed, packed.T)
            else:
                other = jnp.where(row <= col, packed, packed.T)
                other = jnp.where(row == col, diagonals[m // 2 : m // 2 + 1], other)
            square = acc[e, rows_at(kept, m), 0:DK] + other
            lefts.append(jnp.concatenate(split(square), axis=1))
            targets.append(
                acc[e, rows_at(kept, m), DK:] + pack_in[e, m * DK : (m + 1) * DK].astype(F32)
            )
            states.append(init_buf[2 * m + e])
        for step in range(ITERS):
            for m in range(OWN):
                high, low = split(states[m])
                right = jnp.concatenate(
                    [jnp.concatenate([high, low], axis=1), jnp.concatenate([high, zero], axis=1)],
                    axis=0,
                )
                product = jnp.dot(lefts[m], right, preferred_element_type=F32)
                product = product[:, 0:DK] + product[:, DK:]
                states[m] = states[m] + scale * (targets[m] - product)
        for m in range(OWN):
            final[e, side, m] = states[m].astype(BF16)
        remote(
            final.at[e, side], final.at[e, side], final_send.at[e], final_sem.at[e], twin
        ).start()

    def read_out(e, source, which):
        meta = meta_buf[first + stride * source, e]
        names = memories + (which * OWN).astype(F32)
        weight = jnp.where(meta[1:2] == names, meta[3:4], 0.0) + jnp.where(
            meta[2:3] == names, meta[4:5], 0.0
        )
        weight = jnp.concatenate([weight, jnp.zeros((DK - MEM, DK), F32)], axis=0).T
        matrices = jnp.concatenate([final[e, which, m] for m in range(OWN)], axis=1)
        routed = jnp.dot(q_buf[e, source], matrices, preferred_element_type=F32)
        total = jnp.zeros((DK, DK), F32)
        for m in range(OWN):
            piece = routed[:, m * DK : (m + 1) * DK].astype(BF16).astype(F32)
            total = total + weight[:, m : m + 1] * piece
        return total

    for e in range(2):
        part[e, place] = read_out(e, place, side)

        def begin(i, c):
            source = (place + PAIRS - offset(i, PAIRS)) % PAIRS
            slot = q_buf.at[e, source]
            remote(slot, slot, q_send, q_sem.at[e, source], me).wait_recv()
            part[e, source] = read_out(e, source, side)
            return c

        lax.fori_loop(0, PAIRS - 1, begin, 0)

    other_side = 1 - side
    backs = []
    for e in range(2):
        arriving = final.at[e, other_side]
        remote(arriving, arriving, final_send.at[e], final_sem.at[e], twin).wait_recv()
        here = columns(2 * pair + e)

        def answer(i, c):
            source = (place + PAIRS - offset(i, PAIRS)) % PAIRS
            res[e, source] = (part[e, source] + read_out(e, source, other_side)).astype(BF16)
            remote(
                res.at[e, source], out_ref.at[:, here], out_send, out_sem,
                base + first + stride * source,
            ).start()
            return c

        lax.fori_loop(0, PAIRS - 1, answer, 0)
        res[e, place] = (part[e, place] + read_out(e, place, other_side)).astype(BF16)
        back = pltpu.make_async_copy(res.at[e, place], out_ref.at[:, here], own_sem.at[e])
        back.start()
        backs.append(back)

    for back in backs:
        back.wait()
    for e in range(2):
        leaving = final.at[e, side]
        remote(leaving, leaving, final_send.at[e], final_sem.at[e], twin).wait_send()
    count = 2 * (PAIRS - 1)
    answers = out_ref.at[:, pl.ds(0, count * DK)]
    remote(answers, answers, out_send, out_sem, me).wait()
    remote(answers, answers, q_send, q_sem.at[0, 0], me).wait_send()
    slots = kv_buf.at[:, pl.ds(0, half - 1)]
    remote(slots, slots, kv_send, kv_sem.at[0, 0], me).wait_send()
    remote(meta_slots, meta_slots, meta_send, meta_sem, me).wait_send()
    remote(init_slots, init_slots, init_send, init_sem, me).wait_send()


def on_device(queries, key_rows, value_rows, step_size, routes, route_weight, init_state):
    n = lax.axis_size("tok")
    half = n // 2
    rows = queries.shape[0]
    scale = 4.0 / math.sqrt(rows * n)
    rates = step_size.T.astype(F32)[:, None, :]
    shared = jnp.concatenate(
        [routes.T.astype(F32), route_weight.T, jnp.zeros((3, rows), F32)], axis=0
    )
    meta = jnp.concatenate([rates, jnp.broadcast_to(shared, (H, 7, rows))], axis=1)
    dma = pltpu.SemaphoreType.DMA
    return pl.pallas_call(
        functools.partial(kernel, n, scale),
        out_shape=jax.ShapeDtypeStruct(queries.shape, BF16),
        in_specs=[pl.BlockSpec(memory_space=pl.ANY)] * 3
        + [pl.BlockSpec(memory_space=pltpu.VMEM)]
        + [pl.BlockSpec(memory_space=pl.ANY)],
        out_specs=pl.BlockSpec(memory_space=pltpu.VMEM),
        scratch_shapes=[
            pltpu.VMEM((2, half, 2, rows, DK), BF16),
            pltpu.VMEM((half, 2, 8, rows), F32),
            pltpu.VMEM((2, PAIRS, rows, DK), BF16),
            pltpu.VMEM((2 * OWN, DK, DK), F32),
            pltpu.VMEM((2, MEM * DK, 2 * DK), F32),
            pltpu.VMEM((2, PACKED, DK), BF16),
            pltpu.VMEM((2, PACKED, DK), BF16),
            pltpu.VMEM((2, 2, OWN, DK, DK), BF16),
            pltpu.VMEM((2, PAIRS, rows, DK), F32),
            pltpu.VMEM((2, PAIRS, rows, DK), BF16),
            dma((2, half)), dma, dma((2, PAIRS)), dma, dma((2,)), dma((2,)), dma,
            dma, dma, dma, dma, dma((2,)), dma((2,)), dma, dma((8,)),
        ],
        compiler_params=pltpu.CompilerParams(
            collective_id=0, has_side_effects=True, vmem_limit_bytes=60 * 1024 * 1024
        ),
    )(queries, key_rows, value_rows, meta, init_state)


def solution(mesh):
    tokens = P(("groups", "tok"), None)
    return jax.shard_map(
        on_device,
        mesh=mesh,
        in_specs=(tokens,) * 6 + (P("tok", None, None),),
        out_specs=tokens,
        check_vma=False,
    )
```

```python
import functools
import math

import jax
import jax.numpy as jnp
from jax import lax
from jax.experimental import pallas as pl
from jax.experimental.pallas import tpu as pltpu
from jax.sharding import PartitionSpec as P

MEM = 8
H = 16
DK = 128
ITERS = 3
PAIRS = H // 2
OWN = MEM // 2
PARTS = OWN // 2
PACKED = 3 * DK + 16
MESH = pl.DeviceIdType.MESH
F32 = jnp.float32
BF16 = jnp.bfloat16


def split(x):
    high = x.astype(BF16)
    return high, (x - high.astype(F32)).astype(BF16)


def kernel(
    n, scale, q_hbm, k_hbm, v_hbm, rate_hbm, route_hbm, weight_hbm, init_hbm, out_ref,
    q_ref, k_ref, v_ref, init_ref, rate_in, route_in, weight_in, meta_ref,
    kv_buf, meta_buf, q_buf, init_buf, acc, pack_out, pack_in, final, part, res,
    kv_sem, meta_sem, q_sem, init_sem, pack_sem, final_sem, out_sem,
    kv_send, meta_send, q_send, init_send, pack_send, final_send, out_send, own_sem,
):
    per_dev = MEM * H // n
    blocks = H // per_dev
    half = n // 2
    stride = max(1, blocks // 8)
    group = lax.axis_index("groups")
    me = lax.axis_index("tok")
    side = me // half
    base = side * half
    local = me % half
    twin = (me + half) % n
    slot_of_me = local // blocks
    place = (local // stride) % PAIRS
    first = (local // (PAIRS * stride)) * (PAIRS * stride) + local % stride

    def pair_of(l):
        if per_dev >= 2:
            pairs = per_dev // 2
            return (l % blocks) * pairs + (l // blocks) % pairs
        return (l % blocks) // 2

    def columns(h):
        return pl.ds(pl.multiple_of(h * DK, DK), DK)

    def offset(i, count):
        return count // 2 + (1 - 2 * (i % 2)) * ((i + 1) // 2)

    def remote(src, dst, send, recv, p):
        return pltpu.make_async_remote_copy(
            src_ref=src, dst_ref=dst, send_sem=send, recv_sem=recv,
            device_id=(group, p), device_id_type=MESH,
        )

    small = [
        pltpu.make_async_copy(src, dst, own_sem.at[i])
        for i, (src, dst) in enumerate(
            [
                (rate_hbm, rate_in), (route_hbm, route_in), (weight_hbm, weight_in),
                (k_hbm, k_ref), (v_hbm, v_ref), (init_hbm, init_ref), (q_hbm, q_ref),
            ]
        )
    ]
    for copy in small:
        copy.start()
    barrier = pltpu.get_barrier_semaphore()

    def greet(i, c):
        pl.semaphore_signal(
            barrier, inc=1, device_id=(group, base + (local + 1 + i) % half),
            device_id_type=MESH,
        )
        return c

    lax.fori_loop(0, half - 1, greet, 0)
    pl.semaphore_signal(barrier, inc=1, device_id=(group, twin), device_id_type=MESH)

    for copy in small:
        copy.wait()
    rates = rate_in[...].astype(F32)
    shared = [route_in[...].astype(F32), weight_in[...], jnp.zeros((3, DK), F32)]
    for h in range(H):
        meta_ref[h] = jnp.concatenate([rates[h : h + 1]] + shared, axis=0)
    pair = pair_of(local)
    own = [pltpu.make_async_copy(meta_ref.at[pl.ds(2 * pair, 2)], meta_buf.at[local], own_sem.at[0])]
    for e in range(2):
        here = columns(2 * pair + e)
        own += [
            pltpu.make_async_copy(k_ref.at[:, here], kv_buf.at[e, local, 0], own_sem.at[1 + 3 * e]),
            pltpu.make_async_copy(v_ref.at[:, here], kv_buf.at[e, local, 1], own_sem.at[2 + 3 * e]),
            pltpu.make_async_copy(q_ref.at[:, here], q_buf.at[e, place], own_sem.at[3 + 3 * e]),
        ]
    if per_dev >= 2:
        own.append(
            pltpu.make_async_copy(
                init_ref.at[pl.ds(2 * (slot_of_me % (per_dev // 2)), 2)],
                init_buf.at[pl.ds(2 * slot_of_me, 2)], own_sem.at[7],
            )
        )
    else:
        own.append(
            pltpu.make_async_copy(
                init_ref.at[0], init_buf.at[2 * slot_of_me + local % 2], own_sem.at[7]
            )
        )
    for copy in own:
        copy.start()
    pl.semaphore_wait(barrier, half)

    for e in range(2):
        def send_kv(i, c):
            l = (local + offset(i, half)) % half
            p = base + l
            h = 2 * pair_of(l) + e
            if e == 0:
                remote(
                    meta_ref.at[pl.ds(2 * pair_of(l), 2)], meta_buf.at[local],
                    meta_send, meta_sem, p,
                ).start()
            sem = kv_sem.at[e, local]
            remote(k_ref.at[:, columns(h)], kv_buf.at[e, local, 0], kv_send, sem, p).start()
            remote(v_ref.at[:, columns(h)], kv_buf.at[e, local, 1], kv_send, sem, p).start()
            return c

        lax.fori_loop(0, half - 1, send_kv, 0)

    if per_dev >= 2:
        def send_init(i, c):
            to = (slot_of_me + 1 + i) % OWN
            remote(
                init_ref.at[pl.ds(2 * (to % (per_dev // 2)), 2)],
                init_buf.at[pl.ds(2 * slot_of_me, 2)], init_send, init_sem,
                base + to * blocks + local % blocks,
            ).start()
            return c

        lax.fori_loop(0, OWN - 1, send_init, 0)
        init_slots = init_buf.at[pl.ds(0, 2 * OWN - 2)]
    else:
        mine = 2 * slot_of_me + local % 2

        def send_init(i, c):
            to = (mine + 1 + i) % (2 * OWN)
            remote(
                init_ref.at[0], init_buf.at[mine], init_send, init_sem,
                base + (to // 2) * blocks + (local % blocks) // 2 * 2 + to % 2,
            ).start()
            return c

        lax.fori_loop(0, 2 * OWN - 1, send_init, 0)
        init_slots = init_buf.at[pl.ds(0, 2 * OWN - 1)]

    for copy in own:
        copy.wait()
    meta_slots = meta_buf.at[pl.ds(0, half - 1)]
    remote(meta_slots, meta_slots, meta_send, meta_sem, me).wait_recv()
    memories = lax.broadcasted_iota(jnp.int32, (MEM, DK), 0).astype(F32)
    row = lax.broadcasted_iota(jnp.int32, (DK, DK), 0)
    col = lax.broadcasted_iota(jnp.int32, (DK, DK), 1)

    def gradient(e, source, fresh):
        meta = meta_buf[source, e]
        picked = (meta[1:2] == memories) | (meta[2:3] == memories)
        keys = kv_buf[e, source, 0].astype(F32)
        keys_t = keys.T
        inverse_row = 1.0 / jnp.sqrt(jnp.sum(keys_t * keys_t, axis=0, keepdims=True) + 1e-06)
        inverse_col = 1.0 / jnp.sqrt(jnp.sum(keys * keys, axis=1, keepdims=True) + 1e-06)
        unit = (keys * inverse_col).astype(BF16)
        right = jnp.concatenate([unit, kv_buf[e, source, 1]], axis=1)
        right = jnp.concatenate([right, right], axis=0)
        both = jnp.concatenate(split(keys_t * (inverse_row * meta[0:1])), axis=1)
        rate = picked.astype(F32)
        rate = jnp.concatenate([rate, rate], axis=1).astype(BF16)
        for m in range(MEM):
            rows = pl.ds(m * DK, DK)
            term = jnp.dot(both * rate[m : m + 1], right, preferred_element_type=F32)
            acc[e, rows, :] = term if fresh else acc[e, rows, :] + term

    away = (1 - side) * (OWN * DK)
    kept = side * (OWN * DK)

    def rows_at(start, m):
        return pl.ds(pl.multiple_of(start + m * DK, DK), DK)

    def packs(e, t):
        return remote(
            pack_out.at[e, t], pack_in.at[e, t], pack_send.at[e, t], pack_sem.at[e, t], twin
        )

    def finals(e, t, which):
        states = final.at[e, which, pl.ds(2 * t, 2)]
        return remote(states, states, final_send.at[e, t], final_sem.at[e, t], twin)

    for e in range(2):
        gradient(e, local, True)

        def arrive(i, c):
            source = (local + half - offset(i, half)) % half
            slot = kv_buf.at[e, source]
            remote(slot, slot, kv_send, kv_sem.at[e, source], me).wait_recv()
            gradient(e, source, False)
            return c

        lax.fori_loop(0, half - 1, arrive, 0)
        for t in range(PARTS):
            for m in range(2):
                pack_out[e, t, m * DK : (m + 1) * DK] = acc[
                    e, rows_at(away, 2 * t + m), DK:
                ].astype(BF16)
            lower = acc[e, rows_at(away, 2 * t), 0:DK]
            upper = acc[e, rows_at(away, 2 * t + 1), 0:DK]
            pack_out[e, t, 2 * DK : 3 * DK] = jnp.where(row >= col, lower, upper).astype(BF16)
            diagonal = jnp.sum(jnp.where(row == col, upper, 0.0), axis=0, keepdims=True)
            pack_out[e, t, 3 * DK :] = jnp.broadcast_to(diagonal, (16, DK)).astype(BF16)
            packs(e, t).start()
        if e == 1:
            for e2 in range(2):
                def send_q(i, c):
                    l = first + stride * ((place + offset(i, PAIRS)) % PAIRS)
                    remote(
                        q_ref.at[:, columns(2 * pair_of(l) + e2)], q_buf.at[e2, place],
                        q_send, q_sem.at[e2, place], base + l,
                    ).start()
                    return c

                lax.fori_loop(0, PAIRS - 1, send_q, 0)

    remote(init_slots, init_slots, init_send, init_sem, me).wait_recv()
    zero = jnp.zeros((DK, DK), BF16)
    for e in range(2):
        for t in range(PARTS):
            packs(e, t).wait()
            packed = pack_in[e, t, 2 * DK : 3 * DK].astype(F32)
            flipped = packed.T
            diagonal = pack_in[e, t, 3 * DK :].astype(F32)[0:1]
            others = [
                jnp.where(row >= col, packed, flipped),
                jnp.where(row == col, diagonal, jnp.where(row < col, packed, flipped)),
            ]
            lefts, targets, states = [], [], []
            for m in range(2):
                rows = rows_at(kept, 2 * t + m)
                lefts.append(jnp.concatenate(split(acc[e, rows, 0:DK] + others[m]), axis=1))
                targets.append(
                    acc[e, rows, DK:] + pack_in[e, t, m * DK : (m + 1) * DK].astype(F32)
                )
                states.append(init_buf[2 * (2 * t + m) + e])
            for step in range(ITERS):
                for m in range(2):
                    high, low = split(states[m])
                    right = jnp.concatenate(
                        [
                            jnp.concatenate([high, low], axis=1),
                            jnp.concatenate([high, zero], axis=1),
                        ],
                        axis=0,
                    )
                    product = jnp.dot(lefts[m], right, preferred_element_type=F32)
                    product = product[:, 0:DK] + product[:, DK:]
                    states[m] = states[m] + scale * (targets[m] - product)
            for m in range(2):
                final[e, side, 2 * t + m] = states[m].astype(BF16)
            finals(e, t, side).start()

    def read_out(e, source, which):
        meta = meta_buf[first + stride * source, e]
        names = memories + (which * OWN).astype(F32)
        weight = jnp.where(meta[1:2] == names, meta[3:4], 0.0) + jnp.where(
            meta[2:3] == names, meta[4:5], 0.0
        )
        weight = jnp.concatenate([weight, jnp.zeros((DK - MEM, DK), F32)], axis=0).T
        matrices = jnp.concatenate([final[e, which, m] for m in range(OWN)], axis=1)
        routed = jnp.dot(q_buf[e, source], matrices, preferred_element_type=F32)
        total = jnp.zeros((DK, DK), F32)
        for m in range(OWN):
            piece = routed[:, m * DK : (m + 1) * DK].astype(BF16).astype(F32)
            total = total + weight[:, m : m + 1] * piece
        return total

    for e in range(2):
        part[e, place] = read_out(e, place, side)

        def begin(i, c):
            source = (place + PAIRS - offset(i, PAIRS)) % PAIRS
            slot = q_buf.at[e, source]
            remote(slot, slot, q_send, q_sem.at[e, source], me).wait_recv()
            part[e, source] = read_out(e, source, side)
            return c

        lax.fori_loop(0, PAIRS - 1, begin, 0)

    other_side = 1 - side
    backs = []
    for e in range(2):
        for t in range(PARTS):
            finals(e, t, other_side).wait_recv()
        here = columns(2 * pair + e)

        def answer(i, c):
            source = (place + PAIRS - offset(i, PAIRS)) % PAIRS
            res[e, source] = (part[e, source] + read_out(e, source, other_side)).astype(BF16)
            remote(
                res.at[e, source], out_ref.at[:, here], out_send, out_sem,
                base + first + stride * source,
            ).start()
            return c

        lax.fori_loop(0, PAIRS - 1, answer, 0)
        res[e, place] = (part[e, place] + read_out(e, place, other_side)).astype(BF16)
        back = pltpu.make_async_copy(res.at[e, place], out_ref.at[:, here], own_sem.at[e])
        back.start()
        backs.append(back)

    for back in backs:
        back.wait()
    for e in range(2):
        for t in range(PARTS):
            finals(e, t, side).wait_send()
    count = 2 * (PAIRS - 1)
    answers = out_ref.at[:, pl.ds(0, count * DK)]
    remote(answers, answers, out_send, out_sem, me).wait()
    remote(answers, answers, q_send, q_sem.at[0, 0], me).wait_send()
    slots = kv_buf.at[:, pl.ds(0, half - 1)]
    remote(slots, slots, kv_send, kv_sem.at[0, 0], me).wait_send()
    remote(meta_slots, meta_slots, meta_send, meta_sem, me).wait_send()
    remote(init_slots, init_slots, init_send, init_sem, me).wait_send()


def on_device(queries, key_rows, value_rows, step_size, routes, route_weight, init_state):
    n = lax.axis_size("tok")
    half = n // 2
    rows = queries.shape[0]
    scale = 4.0 / math.sqrt(rows * n)
    dma = pltpu.SemaphoreType.DMA
    return pl.pallas_call(
        functools.partial(kernel, n, scale),
        out_shape=jax.ShapeDtypeStruct(queries.shape, BF16),
        in_specs=[pl.BlockSpec(memory_space=pl.ANY)] * 7,
        out_specs=pl.BlockSpec(memory_space=pl.ANY),
        scratch_shapes=[
            pltpu.VMEM(queries.shape, BF16),
            pltpu.VMEM(queries.shape, BF16),
            pltpu.VMEM(queries.shape, BF16),
            pltpu.VMEM(init_state.shape, F32),
            pltpu.VMEM((H, rows), BF16),
            pltpu.VMEM((2, rows), jnp.int32),
            pltpu.VMEM((2, rows), F32),
            pltpu.VMEM((H, 8, rows), F32),
            pltpu.VMEM((2, half, 2, rows, DK), BF16),
            pltpu.VMEM((half, 2, 8, rows), F32),
            pltpu.VMEM((2, PAIRS, rows, DK), BF16),
            pltpu.VMEM((2 * OWN, DK, DK), F32),
            pltpu.VMEM((2, MEM * DK, 2 * DK), F32),
            pltpu.VMEM((2, PARTS, PACKED, DK), BF16),
            pltpu.VMEM((2, PARTS, PACKED, DK), BF16),
            pltpu.VMEM((2, 2, OWN, DK, DK), BF16),
            pltpu.VMEM((2, PAIRS, rows, DK), F32),
            pltpu.VMEM((2, PAIRS, rows, DK), BF16),
            dma((2, half)), dma, dma((2, PAIRS)), dma, dma((2, PARTS)), dma((2, PARTS)), dma,
            dma, dma, dma, dma, dma((2, PARTS)), dma((2, PARTS)), dma, dma((8,)),
        ],
        compiler_params=pltpu.CompilerParams(
            collective_id=0, has_side_effects=True, vmem_limit_bytes=40 * 1024 * 1024
        ),
    )(*(pltpu.with_memory_space_constraint(x, pltpu.HBM) for x in (queries, key_rows, value_rows, step_size.T, routes.T, route_weight.T, init_state)))


def solution(mesh):
    tokens = P(("groups", "tok"), None)
    return jax.shard_map(
        on_device,
        mesh=mesh,
        in_specs=(tokens,) * 6 + (P("tok", None, None),),
        out_specs=tokens,
        check_vma=False,
    )
```

```python
import functools
import math

import jax
import jax.numpy as jnp
from jax import lax
from jax.experimental import pallas as pl
from jax.experimental.pallas import tpu as pltpu
from jax.sharding import PartitionSpec as P

MEM = 8
H = 16
DK = 128
ITERS = 3
PAIRS = H // 2
OWN = MEM // 2
PARTS = OWN // 2
PACKED = 3 * DK + 16
MESH = pl.DeviceIdType.MESH
F32 = jnp.float32
BF16 = jnp.bfloat16


def split(x):
    high = x.astype(BF16)
    return high, (x - high.astype(F32)).astype(BF16)


def kernel(
    n, scale, q_hbm, k_hbm, v_hbm, rate_hbm, route_hbm, weight_hbm, init_hbm, out_ref,
    q_ref, k_ref, v_ref, init_ref, rate_in, route_in, weight_in, meta_ref,
    kv_buf, meta_buf, q_buf, init_buf, acc, pack_out, pack_in, final, part, res, wide,
    kv_sem, meta_sem, q_sem, init_sem, pack_sem, final_sem, out_sem,
    kv_send, meta_send, q_send, init_send, pack_send, final_send, out_send, own_sem,
):
    per_dev = MEM * H // n
    blocks = H // per_dev
    half = n // 2
    stride = max(1, blocks // 8)
    group = lax.axis_index("groups")
    me = lax.axis_index("tok")
    side = me // half
    base = side * half
    local = me % half
    twin = (me + half) % n
    slot_of_me = local // blocks
    place = (local // stride) % PAIRS
    first = (local // (PAIRS * stride)) * (PAIRS * stride) + local % stride

    def pair_of(l):
        if per_dev >= 2:
            pairs = per_dev // 2
            return (l % blocks) * pairs + (l // blocks) % pairs
        return (l % blocks) // 2

    def columns(h):
        return pl.ds(pl.multiple_of(h * DK, DK), DK)

    def offset(i, count):
        return count // 2 + (1 - 2 * (i % 2)) * ((i + 1) // 2)

    def remote(src, dst, send, recv, p):
        return pltpu.make_async_remote_copy(
            src_ref=src, dst_ref=dst, send_sem=send, recv_sem=recv,
            device_id=(group, p), device_id_type=MESH,
        )

    small = [
        pltpu.make_async_copy(src, dst, own_sem.at[i])
        for i, (src, dst) in enumerate(
            [
                (rate_hbm, rate_in), (route_hbm, route_in), (weight_hbm, weight_in),
                (k_hbm, k_ref), (v_hbm, v_ref), (init_hbm, init_ref), (q_hbm, q_ref),
            ]
        )
    ]
    for copy in small:
        copy.start()
    barrier = pltpu.get_barrier_semaphore()

    def greet(i, c):
        pl.semaphore_signal(
            barrier, inc=1, device_id=(group, base + (local + 1 + i) % half),
            device_id_type=MESH,
        )
        return c

    lax.fori_loop(0, half - 1, greet, 0)
    pl.semaphore_signal(barrier, inc=1, device_id=(group, twin), device_id_type=MESH)

    for copy in small:
        copy.wait()
    rates = rate_in[...].astype(F32)
    shared = [route_in[...].astype(F32), weight_in[...], jnp.zeros((3, DK), F32)]
    for h in range(H):
        meta_ref[h] = jnp.concatenate([rates[h : h + 1]] + shared, axis=0)
    pair = pair_of(local)
    own = [pltpu.make_async_copy(meta_ref.at[pl.ds(2 * pair, 2)], meta_buf.at[local], own_sem.at[0])]
    for e in range(2):
        here = columns(2 * pair + e)
        own += [
            pltpu.make_async_copy(k_ref.at[:, here], kv_buf.at[e, local, 0], own_sem.at[1 + 3 * e]),
            pltpu.make_async_copy(v_ref.at[:, here], kv_buf.at[e, local, 1], own_sem.at[2 + 3 * e]),
            pltpu.make_async_copy(q_ref.at[:, here], q_buf.at[e, place], own_sem.at[3 + 3 * e]),
        ]
    if per_dev >= 2:
        own.append(
            pltpu.make_async_copy(
                init_ref.at[pl.ds(2 * (slot_of_me % (per_dev // 2)), 2)],
                init_buf.at[pl.ds(2 * slot_of_me, 2)], own_sem.at[7],
            )
        )
    else:
        own.append(
            pltpu.make_async_copy(
                init_ref.at[0], init_buf.at[2 * slot_of_me + local % 2], own_sem.at[7]
            )
        )
    for copy in own:
        copy.start()
    pl.semaphore_wait(barrier, half)

    for e in range(2):
        def send_kv(i, c):
            l = (local + offset(i, half)) % half
            p = base + l
            h = 2 * pair_of(l) + e
            if e == 0:
                remote(
                    meta_ref.at[pl.ds(2 * pair_of(l), 2)], meta_buf.at[local],
                    meta_send, meta_sem, p,
                ).start()
            sem = kv_sem.at[e, local]
            remote(k_ref.at[:, columns(h)], kv_buf.at[e, local, 0], kv_send, sem, p).start()
            remote(v_ref.at[:, columns(h)], kv_buf.at[e, local, 1], kv_send, sem, p).start()
            return c

        lax.fori_loop(0, half - 1, send_kv, 0)

    if per_dev >= 2:
        def send_init(i, c):
            to = (slot_of_me + 1 + i) % OWN
            remote(
                init_ref.at[pl.ds(2 * (to % (per_dev // 2)), 2)],
                init_buf.at[pl.ds(2 * slot_of_me, 2)], init_send, init_sem,
                base + to * blocks + local % blocks,
            ).start()
            return c

        lax.fori_loop(0, OWN - 1, send_init, 0)
        init_slots = init_buf.at[pl.ds(0, 2 * OWN - 2)]
    else:
        mine = 2 * slot_of_me + local % 2

        def send_init(i, c):
            to = (mine + 1 + i) % (2 * OWN)
            remote(
                init_ref.at[0], init_buf.at[mine], init_send, init_sem,
                base + (to // 2) * blocks + (local % blocks) // 2 * 2 + to % 2,
            ).start()
            return c

        lax.fori_loop(0, 2 * OWN - 1, send_init, 0)
        init_slots = init_buf.at[pl.ds(0, 2 * OWN - 1)]

    for copy in own:
        copy.wait()
    meta_slots = meta_buf.at[pl.ds(0, half - 1)]
    remote(meta_slots, meta_slots, meta_send, meta_sem, me).wait_recv()
    memories = lax.broadcasted_iota(jnp.int32, (MEM, DK), 0).astype(F32)
    row = lax.broadcasted_iota(jnp.int32, (DK, DK), 0)
    col = lax.broadcasted_iota(jnp.int32, (DK, DK), 1)

    def gradient(e, source, fresh):
        meta = meta_buf[source, e]
        picked = (meta[1:2] == memories) | (meta[2:3] == memories)
        keys = kv_buf[e, source, 0].astype(F32)
        keys_t = keys.T
        inverse_row = 1.0 / jnp.sqrt(jnp.sum(keys_t * keys_t, axis=0, keepdims=True) + 1e-06)
        inverse_col = 1.0 / jnp.sqrt(jnp.sum(keys * keys, axis=1, keepdims=True) + 1e-06)
        unit = (keys * inverse_col).astype(BF16)
        right = jnp.concatenate([unit, kv_buf[e, source, 1]], axis=1)
        right = jnp.concatenate([right, right], axis=0)
        both = jnp.concatenate(split(keys_t * (inverse_row * meta[0:1])), axis=1)
        rate = picked.astype(F32)
        rate = jnp.concatenate([rate, rate], axis=1).astype(BF16)
        for m in range(MEM):
            rows = pl.ds(m * DK, DK)
            term = jnp.dot(both * rate[m : m + 1], right, preferred_element_type=F32)
            acc[e, rows, :] = term if fresh else acc[e, rows, :] + term

    away = (1 - side) * (OWN * DK)
    kept = side * (OWN * DK)

    def rows_at(start, m):
        return pl.ds(pl.multiple_of(start + m * DK, DK), DK)

    def spread(source, c):
        meta = meta_buf[first + stride * source, 0]
        weight = jnp.where(meta[1:2] == memories, meta[3:4], 0.0) + jnp.where(
            meta[2:3] == memories, meta[4:5], 0.0
        )
        weight = jnp.concatenate([weight, jnp.zeros((DK - MEM, DK), F32)], axis=0).T
        for m in range(MEM):
            wide[source, m] = jnp.broadcast_to(weight[:, m : m + 1], (DK, DK))
        return c

    def packs(e, t):
        return remote(
            pack_out.at[e, t], pack_in.at[e, t], pack_send.at[e, t], pack_sem.at[e, t], twin
        )

    def finals(e, t, which):
        states = final.at[e, which, pl.ds(2 * t, 2)]
        return remote(states, states, final_send.at[e, t], final_sem.at[e, t], twin)

    for e in range(2):
        gradient(e, local, True)

        def arrive(i, c):
            source = (local + half - offset(i, half)) % half
            slot = kv_buf.at[e, source]
            remote(slot, slot, kv_send, kv_sem.at[e, source], me).wait_recv()
            gradient(e, source, False)
            return c

        lax.fori_loop(0, half - 1, arrive, 0)
        for t in range(PARTS):
            for m in range(2):
                pack_out[e, t, m * DK : (m + 1) * DK] = acc[
                    e, rows_at(away, 2 * t + m), DK:
                ].astype(BF16)
            lower = acc[e, rows_at(away, 2 * t), 0:DK]
            upper = acc[e, rows_at(away, 2 * t + 1), 0:DK]
            pack_out[e, t, 2 * DK : 3 * DK] = jnp.where(row >= col, lower, upper).astype(BF16)
            diagonal = jnp.sum(jnp.where(row == col, upper, 0.0), axis=0, keepdims=True)
            pack_out[e, t, 3 * DK :] = jnp.broadcast_to(diagonal, (16, DK)).astype(BF16)
            packs(e, t).start()
        if e == 1:
            for e2 in range(2):
                def send_q(i, c):
                    l = first + stride * ((place + offset(i, PAIRS)) % PAIRS)
                    remote(
                        q_ref.at[:, columns(2 * pair_of(l) + e2)], q_buf.at[e2, place],
                        q_send, q_sem.at[e2, place], base + l,
                    ).start()
                    return c

                lax.fori_loop(0, PAIRS - 1, send_q, 0)

    lax.fori_loop(0, PAIRS, spread, 0)
    remote(init_slots, init_slots, init_send, init_sem, me).wait_recv()
    zero = jnp.zeros((DK, DK), BF16)
    for e in range(2):
        for t in range(PARTS):
            packs(e, t).wait()
            packed = pack_in[e, t, 2 * DK : 3 * DK].astype(F32)
            flipped = packed.T
            diagonal = pack_in[e, t, 3 * DK :].astype(F32)[0:1]
            others = [
                jnp.where(row >= col, packed, flipped),
                jnp.where(row == col, diagonal, jnp.where(row < col, packed, flipped)),
            ]
            lefts, targets, states = [], [], []
            for m in range(2):
                rows = rows_at(kept, 2 * t + m)
                lefts.append(jnp.concatenate(split(acc[e, rows, 0:DK] + others[m]), axis=1))
                targets.append(
                    acc[e, rows, DK:] + pack_in[e, t, m * DK : (m + 1) * DK].astype(F32)
                )
                states.append(init_buf[2 * (2 * t + m) + e])
            for step in range(ITERS):
                for m in range(2):
                    high, low = split(states[m])
                    right = jnp.concatenate(
                        [
                            jnp.concatenate([high, low], axis=1),
                            jnp.concatenate([high, zero], axis=1),
                        ],
                        axis=0,
                    )
                    product = jnp.dot(lefts[m], right, preferred_element_type=F32)
                    product = product[:, 0:DK] + product[:, DK:]
                    states[m] = states[m] + scale * (targets[m] - product)
            for m in range(2):
                final[e, side, 2 * t + m] = states[m].astype(BF16)
            finals(e, t, side).start()

    def read_out(e, source, which):
        matrices = jnp.concatenate([final[e, which, m] for m in range(OWN)], axis=1)
        routed = jnp.dot(q_buf[e, source], matrices, preferred_element_type=F32)
        total = jnp.zeros((DK, DK), F32)
        for m in range(OWN):
            piece = routed[:, m * DK : (m + 1) * DK].astype(BF16).astype(F32)
            total = total + wide[source, which * OWN + m] * piece
        return total

    for e in range(2):
        part[e, place] = read_out(e, place, side)

        def begin(i, c):
            source = (place + PAIRS - offset(i, PAIRS)) % PAIRS
            slot = q_buf.at[e, source]
            remote(slot, slot, q_send, q_sem.at[e, source], me).wait_recv()
            part[e, source] = read_out(e, source, side)
            return c

        lax.fori_loop(0, PAIRS - 1, begin, 0)

    other_side = 1 - side
    backs = []
    for e in range(2):
        for t in range(PARTS):
            finals(e, t, other_side).wait_recv()
        here = columns(2 * pair + e)

        def answer(i, c):
            source = (place + PAIRS - offset(i, PAIRS)) % PAIRS
            res[e, source] = (part[e, source] + read_out(e, source, other_side)).astype(BF16)
            remote(
                res.at[e, source], out_ref.at[:, here], out_send, out_sem,
                base + first + stride * source,
            ).start()
            return c

        lax.fori_loop(0, PAIRS - 1, answer, 0)
        res[e, place] = (part[e, place] + read_out(e, place, other_side)).astype(BF16)
        back = pltpu.make_async_copy(res.at[e, place], out_ref.at[:, here], own_sem.at[e])
        back.start()
        backs.append(back)

    for back in backs:
        back.wait()
    for e in range(2):
        for t in range(PARTS):
            finals(e, t, side).wait_send()
    count = 2 * (PAIRS - 1)
    answers = out_ref.at[:, pl.ds(0, count * DK)]
    remote(answers, answers, out_send, out_sem, me).wait()
    remote(answers, answers, q_send, q_sem.at[0, 0], me).wait_send()
    slots = kv_buf.at[:, pl.ds(0, half - 1)]
    remote(slots, slots, kv_send, kv_sem.at[0, 0], me).wait_send()
    remote(meta_slots, meta_slots, meta_send, meta_sem, me).wait_send()
    remote(init_slots, init_slots, init_send, init_sem, me).wait_send()


def on_device(queries, key_rows, value_rows, step_size, routes, route_weight, init_state):
    n = lax.axis_size("tok")
    half = n // 2
    rows = queries.shape[0]
    scale = 4.0 / math.sqrt(rows * n)
    dma = pltpu.SemaphoreType.DMA
    return pl.pallas_call(
        functools.partial(kernel, n, scale),
        out_shape=jax.ShapeDtypeStruct(queries.shape, BF16),
        in_specs=[pl.BlockSpec(memory_space=pl.ANY)] * 7,
        out_specs=pl.BlockSpec(memory_space=pl.ANY),
        scratch_shapes=[
            pltpu.VMEM(queries.shape, BF16),
            pltpu.VMEM(queries.shape, BF16),
            pltpu.VMEM(queries.shape, BF16),
            pltpu.VMEM(init_state.shape, F32),
            pltpu.VMEM((H, rows), BF16),
            pltpu.VMEM((2, rows), jnp.int32),
            pltpu.VMEM((2, rows), F32),
            pltpu.VMEM((H, 8, rows), F32),
            pltpu.VMEM((2, half, 2, rows, DK), BF16),
            pltpu.VMEM((half, 2, 8, rows), F32),
            pltpu.VMEM((2, PAIRS, rows, DK), BF16),
            pltpu.VMEM((2 * OWN, DK, DK), F32),
            pltpu.VMEM((2, MEM * DK, 2 * DK), F32),
            pltpu.VMEM((2, PARTS, PACKED, DK), BF16),
            pltpu.VMEM((2, PARTS, PACKED, DK), BF16),
            pltpu.VMEM((2, 2, OWN, DK, DK), BF16),
            pltpu.VMEM((2, PAIRS, rows, DK), F32),
            pltpu.VMEM((2, PAIRS, rows, DK), BF16),
            pltpu.VMEM((PAIRS, MEM, rows, DK), F32),
            dma((2, half)), dma, dma((2, PAIRS)), dma, dma((2, PARTS)), dma((2, PARTS)), dma,
            dma, dma, dma, dma, dma((2, PARTS)), dma((2, PARTS)), dma, dma((8,)),
        ],
        compiler_params=pltpu.CompilerParams(
            collective_id=0, has_side_effects=True, vmem_limit_bytes=40 * 1024 * 1024
        ),
    )(*(pltpu.with_memory_space_constraint(x, pltpu.HBM) for x in (queries, key_rows, value_rows, step_size.T, routes.T, route_weight.T, init_state)))


def solution(mesh):
    tokens = P(("groups", "tok"), None)
    return jax.shard_map(
        on_device,
        mesh=mesh,
        in_specs=(tokens,) * 6 + (P("tok", None, None),),
        out_specs=tokens,
        check_vma=False,
    )
```
